256 devices in a mesh: win: 16 (over z, y_lo), seq: 16 (over x, y_hi, core).
Axes of the slice: x: 4, y: 4 (y_hi: 2, y_lo: 2; y = y_hi * 2 + y_lo), z: 8, core: 2. Of those that a mesh axis runs over, the one named last changes fastest.
Arguments:
- queries: bfloat16 [2, 16, 2048, 2048], P(None, 'win', 'seq'), may hold values from -4.5 to 4.5
- key_states: bfloat16 [2, 16, 2048, 2048], P(None, 'win', 'seq'), may hold values from -4.5 to 4.5
- value_states: bfloat16 [2, 16, 2048, 2048], P(None, 'win', 'seq'), may hold values from -5 to 5
- out_grad: bfloat16 [2, 16, 2048, 2048], P(None, 'win', 'seq'), may hold values from -60 to 60
Outputs:
- query_grad: bfloat16 [2, 16, 2048, 2048], P(None, 'win', 'seq')
- key_grad: bfloat16 [2, 16, 2048, 2048], P(None, 'win', 'seq')
- value_grad: bfloat16 [2, 16, 2048, 2048], P(None, 'win', 'seq')
The draws below stay inside these ranges and needn't reach their ends.
All inputs are finite; a program needn't handle non-finite values.
Results may differ from the reference program's by a relative error of at most 0.0095.
Values may be sent and summed in bfloat16 or wider, within the bound.
A program may use at most 128 MiB of HBM per device.

```python
import jax
import jax.numpy as jnp
from jax import lax

HEADS = 16
HDIM = 128
D = 2048
ROWS = 32
COLS = 64
WTOK = 2048
SAMPLES = 2
WINDOWS = 16


def rough_base(key, salt):
    values = jax.random.normal(jax.random.fold_in(key, salt), (SAMPLES, WINDOWS, WTOK, D), jnp.float32)
    values = jnp.clip(values, -4.5, 4.5)
    return values


def draw_queries(key, part):
    values = rough_base(key, 11)
    return values.astype(jnp.bfloat16)


def draw_key_states(key, part):
    values = rough_base(key, 13)
    return values.astype(jnp.bfloat16)


def block_levels(rng, dims, pieces, low, top_value):
    level = 1.0
    for dim, parts in pieces:
        heights = jax.random.uniform(jax.random.fold_in(jax.random.fold_in(rng, 6), dim), (parts,), jnp.float32, low / len(pieces), top_value / len(pieces))
        level = level * jnp.repeat(jnp.exp(heights), dims[dim] // parts).reshape((-1,) + (1,) * (len(dims) - 1 - dim))
    return level


def scatter_about(key, extent, deviation, limit, cuts=(), held_as=jnp.bfloat16):
    entries = jax.random.normal(key, extent, jnp.float32) * deviation
    if len(cuts) > 0:
        entries = block_levels(key, extent, cuts, -0.22, 0.18) * entries
    return jnp.clip(entries, min=-limit, max=limit).astype(held_as)


def setup_inputs(seed: int = 0) -> dict:
    seeds = jax.random.split(jax.random.key(seed), 5)
    queries = draw_queries(jax.random.fold_in(seeds[4], 71), 0)
    key_states = draw_key_states(jax.random.fold_in(seeds[4], 71), 0)
    value_states = scatter_about(seeds[2], (SAMPLES, WINDOWS, WTOK, D), 1.0, 5.0, ((1, 16), (2, 16)))
    out_grad = scatter_about(seeds[3], (SAMPLES, WINDOWS, WTOK, D), 12.0, 60.0, ((1, 16), (2, 16)))
    return dict(queries=queries, key_states=key_states, value_states=value_states, out_grad=out_grad)


def to_grid(values, windows):
    samples = values.shape[0]
    shaped = values.reshape(samples, windows, ROWS, COLS, -1)
    return shaped.transpose(0, 2, 1, 3, 4).reshape(samples, ROWS, windows * COLS, -1)


def to_windows(token_grid, windows):
    samples = token_grid.shape[0]
    shaped = token_grid.reshape(samples, ROWS, windows, COLS, -1)
    return shaped.transpose(0, 2, 1, 3, 4).reshape(samples, windows, ROWS * COLS, -1)


def window_grads(query_heads, key_heads, value_heads, grad_heads):
    samples_here, tokens, own_heads, head_size = query_heads.shape
    block_rows = min(512, tokens)
    factor = head_size ** -0.5
    query_wide = query_heads.astype(jnp.float32)
    key_wide = key_heads.astype(jnp.float32)
    value_wide = value_heads.astype(jnp.float32)
    grad_wide = grad_heads.astype(jnp.float32)

    def one_block(totals, offset):
        key_total, value_total = totals
        query_block = lax.dynamic_slice_in_dim(query_wide, offset, block_rows, 1)
        grad_block = lax.dynamic_slice_in_dim(grad_wide, offset, block_rows, 1)
        scores = jnp.einsum("bqhd,bkhd->bhqk", query_block, key_wide) * factor
        scores = scores - jnp.max(scores, axis=3, keepdims=True)
        weights = jnp.exp(scores)
        weights = weights / jnp.sum(weights, axis=3, keepdims=True)
        weights_low = weights.astype(jnp.bfloat16).astype(jnp.float32)
        value_total = value_total + jnp.einsum("bhqk,bqhd->bkhd", weights_low, grad_block)
        grad_probs = jnp.einsum("bqhd,bkhd->bhqk", grad_block, value_wide)
        row_dot = jnp.sum(weights * grad_probs, axis=3, keepdims=True)
        grad_scores = (weights * (grad_probs - row_dot) * factor).astype(jnp.bfloat16).astype(jnp.float32)
        query_block_grad = jnp.einsum("bhqk,bkhd->bqhd", grad_scores, key_wide).astype(jnp.bfloat16)
        key_total = key_total + jnp.einsum("bhqk,bqhd->bkhd", grad_scores, query_block)
        return (key_total, value_total), query_block_grad

    starts = jnp.arange(tokens // block_rows, dtype=jnp.int32) * block_rows
    zero_acc = jnp.zeros(query_heads.shape, jnp.float32)
    (key_total, value_total), query_blocks = lax.scan(one_block, (zero_acc, zero_acc), starts)
    query_grad = jnp.moveaxis(query_blocks, 0, 1).reshape(samples_here, tokens, own_heads, head_size)
    return jnp.stack([query_grad, key_total.astype(jnp.bfloat16), value_total.astype(jnp.bfloat16)])


def reference(queries, key_states, value_states, out_grad):
    samples = queries.shape[0]
    windows = queries.shape[1]
    moved_grad = to_windows(jnp.roll(to_grid(out_grad, windows), (-(ROWS // 2), -(COLS // 2)), axis=(1, 2)), windows)

    def as_items(values):
        return values.reshape(samples * windows, 1, ROWS * COLS, HEADS, HDIM)

    def one_window(inputs):
        return window_grads(inputs[0], inputs[1], inputs[2], inputs[3])

    stacked = lax.map(one_window, (as_items(queries), as_items(key_states), as_items(value_states), as_items(moved_grad)))

    def restore(which):
        shifted = stacked[:, which].reshape(samples, windows, ROWS * COLS, HEADS * HDIM)
        return to_windows(jnp.roll(to_grid(shifted, windows), (ROWS // 2, COLS // 2), axis=(1, 2)), windows)

    return restore(0), restore(1), restore(2)
```

```python
import jax
import jax.numpy as jnp
from jax import lax
from jax.experimental import pallas as pl
from jax.experimental.pallas import tpu as pltpu
from jax.sharding import PartitionSpec as P

F32, BF16 = jnp.float32, jnp.bfloat16
MESH = pl.DeviceIdType.MESH
SAMPLES, HEADS, HDIM, D = 2, 16, 128, 2048
WINS, SEQS = 16, 16
TOKENS = 2048
GROUPS, MEMBERS = 4, 4
ROWS_HERE, HALVES, HALF = 2, 2, 32
CHUNK = GROUPS * ROWS_HERE * HALVES * HALF
FACTOR = HDIM**-0.5
LOG2E = 1.4426950408889634


def dot(a, b, ca, cb):
    return lax.dot_general(a, b, (((ca,), (cb,)), ((), ())), preferred_element_type=F32)


def rows_of(block):
    return block.reshape(-1, HDIM)


def kernel(
    q, k, v, g, dq_out, dk_out, dv_out, got, made, key_total, value_total, key_t, weights, products,
    in_sem, in_send, out_sem, out_send,
):
    win = lax.axis_index("win")
    seq = lax.axis_index("seq")
    group, member = lax.div(seq, MEMBERS), lax.rem(seq, MEMBERS)
    west, east = lax.rem(win + WINS - 1, WINS), lax.rem(win + 1, WINS)

    barrier = pltpu.get_barrier_semaphore()

    def greet(n, carry):
        peer = lax.rem(seq + n, SEQS)
        for side in (west, east):
            pl.semaphore_signal(barrier, inc=1, device_id={"win": side, "seq": peer}, device_id_type=MESH)

        @pl.when(n > 0)
        def _():
            pl.semaphore_signal(barrier, inc=1, device_id={"win": win, "seq": peer}, device_id_type=MESH)

        return carry

    lax.fori_loop(0, SEQS, greet, 0)
    pl.semaphore_wait(barrier, 3 * SEQS - 1)

    def send(src, dst, send_sem, recv_sem, to_win, to_seq):
        pltpu.make_async_remote_copy(
            src_ref=src,
            dst_ref=dst,
            send_sem=send_sem,
            recv_sem=recv_sem,
            device_id={"win": to_win, "seq": to_seq},
            device_id_type=MESH,
        ).start()

    def peer_at(n):
        over = lax.rem(n + 1, 4)
        across = lax.rem(n + lax.div(n, 4), 2)
        core = 1 - lax.div(n, 8)
        to_group = lax.rem(group + over, GROUPS)
        to_high = lax.rem(lax.div(member, 2) + across, 2)
        to_core = lax.rem(lax.rem(member, 2) + core, 2)
        return to_group * MEMBERS + to_high * 2 + to_core

    moved_group = lax.rem(group + 2, GROUPS)

    def send_inputs(b):
        def step(n, carry):
            peer = peer_at(n)
            columns = pl.ds(pl.multiple_of(peer * HDIM, HDIM), HDIM)
            send(
                g.at[b, :, 0, :, columns],
                got.at[b, 3, moved_group, member, :, 1],
                in_send.at[b, 4],
                in_sem.at[b],
                west,
                peer,
            )

            @pl.when(n < SEQS - 1)
            def _():
                for a, array in enumerate((q, k, v)):
                    send(
                        array.at[b, :, :, :, columns],
                        got.at[b, a, group, member],
                        in_send.at[b, a],
                        in_sem.at[b],
                        win,
                        peer,
                    )
                send(
                    g.at[b, :, 1, :, columns],
                    got.at[b, 3, moved_group, member, :, 0],
                    in_send.at[b, 3],
                    in_sem.at[b],
                    win,
                    peer,
                )

            return carry

        lax.fori_loop(0, SEQS, step, 0)
        columns = pl.ds(pl.multiple_of(seq * HDIM, HDIM), HDIM)
        for a, array in enumerate((q, k, v)):
            pltpu.make_async_copy(array.at[b, :, :, :, columns], got.at[b, a, group, member], in_sem.at[b]).start()
        pltpu.make_async_copy(
            g.at[b, :, 1, :, columns], got.at[b, 3, moved_group, member, :, 0], in_sem.at[b]
        ).start()

    my_columns = pl.ds(pl.multiple_of(seq * HDIM, HDIM), HDIM)
    outs = (dq_out, dk_out, dv_out)

    def send_gradient(b, a, to_group, to_member):
        peer = to_group * MEMBERS + to_member
        at_group = lax.rem(to_group + 2, GROUPS)
        here = outs[a].at[b, :, 1, :, my_columns]
        send(
            made.at[b, a, at_group, to_member, :, 1],
            outs[a].at[b, :, 0, :, my_columns],
            out_send.at[b, a, 1],
            out_sem.at[a],
            east,
            peer,
        )

        @pl.when(peer != seq)
        def _():
            send(made.at[b, a, at_group, to_member, :, 0], here, out_send.at[b, a, 0], out_sem.at[a], win, peer)

        @pl.when(peer == seq)
        def _():
            pltpu.make_async_copy(made.at[b, a, at_group, to_member, :, 0], here, out_sem.at[a]).start()

    def grads(b):
        key_total[...] = jnp.zeros_like(key_total)
        value_total[...] = jnp.zeros_like(value_total)
        key_t[...] = rows_of(got[b, 1]).T

        def block(j, carry):
            query = rows_of(got[b, 0, :, j])
            grad = rows_of(got[b, 3, :, j])
            top = jnp.full((8, CHUNK), -jnp.inf, F32)
            for i in range(TOKENS // CHUNK):
                keys = pl.ds(i * CHUNK, CHUNK)
                scores = dot(rows_of(got[b, 1, i]), query, 1, 1)
                weights[keys] = scores
                top = jnp.maximum(top, jnp.max(scores.reshape(-1, 8, CHUNK), axis=0))
            top = jnp.max(top, axis=0, keepdims=True) * (FACTOR * LOG2E)
            total = jnp.zeros((8, CHUNK), F32)
            row_dot = jnp.zeros((8, CHUNK), F32)
            for i in range(TOKENS // CHUNK):
                keys = pl.ds(i * CHUNK, CHUNK)
                weight = jnp.exp2(weights[keys] * (FACTOR * LOG2E) - top)
                product = weight * dot(rows_of(got[b, 2, i]), grad, 1, 1)
                total = total + jnp.sum(weight.reshape(-1, 8, CHUNK), axis=0)
                row_dot = row_dot + jnp.sum(product.reshape(-1, 8, CHUNK), axis=0)
                weights[keys] = weight
                products[keys] = product
            share = 1.0 / jnp.sum(total, axis=0, keepdims=True)
            row_dot = jnp.sum(row_dot, axis=0, keepdims=True) * share * share
            query_grad = jnp.zeros((HDIM, CHUNK), F32)
            for i in range(TOKENS // CHUNK):
                keys = pl.ds(i * CHUNK, CHUNK)
                weight = weights[keys]
                low = (weight * share).astype(BF16)
                score_grad = (products[keys] * share - weight * row_dot).astype(BF16)
                value_total[keys] += dot(low, grad, 1, 0)
                key_total[keys] += dot(score_grad, query, 1, 0)
                query_grad = query_grad + dot(key_t[:, keys], score_grad, 1, 0)
            made[b, 0, :, j] = (query_grad * FACTOR).T.astype(BF16).reshape(GROUPS, ROWS_HERE, HALVES, HALF, HDIM)
            for n in range(GROUPS):
                send_gradient(b, 0, lax.rem(group + n + 1, GROUPS), j)
            return carry

        lax.fori_loop(0, MEMBERS, block, 0)
        whole = (GROUPS, MEMBERS, ROWS_HERE, HALVES, HALF, HDIM)
        made[b, 1] = (key_total[...] * FACTOR).astype(BF16).reshape(whole)
        made[b, 2] = value_total[...].astype(BF16).reshape(whole)

        def step(n, carry):
            peer = peer_at(n)
            for a in (1, 2):
                send_gradient(b, a, lax.div(peer, MEMBERS), lax.rem(peer, MEMBERS))
            return carry

        lax.fori_loop(0, SEQS, step, 0)

    for b in range(SAMPLES):
        send_inputs(b)

    def sample(b, carry):
        pltpu.make_async_copy(got.at[b], got.at[b], in_sem.at[b]).wait()
        grads(b)
        return carry

    lax.fori_loop(0, SAMPLES, sample, 0)

    def all_sent(ref, sem):
        pltpu.make_async_copy(ref, ref, sem).wait()

    others = pl.ds(0, SEQS - 1)
    for a in range(3):
        pltpu.make_async_copy(outs[a], outs[a], out_sem.at[a]).wait()
    for b in range(SAMPLES):
        for a in range(3):
            all_sent(q.at[b, :, :, :, pl.ds(0, (SEQS - 1) * HDIM)], in_send.at[b, a])
        all_sent(q.at[b, :, 0, :, pl.ds(0, (SEQS - 1) * HDIM)], in_send.at[b, 3])
        all_sent(q.at[b, :, 0], in_send.at[b, 4])
        for a in range(3):
            all_sent(q.at[b, :, 0, :, pl.ds(0, (SEQS - 1) * HDIM)], out_send.at[b, a, 0])
            all_sent(q.at[b, :, 0], out_send.at[b, a, 1])


def on_device(queries, key_states, value_states, out_grad):
    shape = (SAMPLES, ROWS_HERE, HALVES, HALF, D)
    arrays = [a.reshape(shape) for a in (queries, key_states, value_states, out_grad)]
    tokens = (GROUPS, MEMBERS, ROWS_HERE, HALVES, HALF, HDIM)
    results = pl.pallas_call(
        kernel,
        out_shape=[jax.ShapeDtypeStruct(shape, BF16)] * 3,
        in_specs=[pl.BlockSpec(memory_space=pltpu.HBM)] * 4,
        out_specs=[pl.BlockSpec(memory_space=pltpu.HBM)] * 3,
        scratch_shapes=[
            pltpu.VMEM((SAMPLES, 4, *tokens), BF16),
            pltpu.VMEM((SAMPLES, 3, *tokens), BF16),
            pltpu.VMEM((TOKENS, HDIM), F32),
            pltpu.VMEM((TOKENS, HDIM), F32),
            pltpu.VMEM((HDIM, TOKENS), BF16),
            pltpu.VMEM((TOKENS, CHUNK), F32),
            pltpu.VMEM((TOKENS, CHUNK), F32),
            pltpu.SemaphoreType.DMA((SAMPLES,)),
            pltpu.SemaphoreType.DMA((SAMPLES, 5)),
            pltpu.SemaphoreType.DMA((3,)),
            pltpu.SemaphoreType.DMA((SAMPLES, 3, 2)),
        ],
        compiler_params=pltpu.CompilerParams(collective_id=0, has_side_effects=True, vmem_limit_bytes=56 * 2**20),
        cost_estimate=pl.CostEstimate(flops=10 * 2 * TOKENS * TOKENS * HDIM, bytes_accessed=7 * 2**20, transcendentals=2 * TOKENS * TOKENS),
        name="window_backward",
    )(*arrays)
    return tuple(r.reshape(queries.shape) for r in results)


def solution(mesh):
    spec = P(None, "win", "seq", None)
    return jax.shard_map(on_device, mesh=mesh, in_specs=(spec,) * 4, out_specs=(spec,) * 3, check_vma=False)
```

```python
import jax
import jax.numpy as jnp
from jax import lax
from jax.experimental import pallas as pl
from jax.experimental.pallas import tpu as pltpu
from jax.sharding import PartitionSpec as P

F32, BF16 = jnp.float32, jnp.bfloat16
MESH = pl.DeviceIdType.MESH
SAMPLES, HEADS, HDIM, D = 2, 16, 128, 2048
WINS, SEQS = 16, 16
TOKENS = 2048
GROUPS, MEMBERS = 4, 4
ROWS_HERE, HALVES, HALF = 2, 2, 32
CHUNK = GROUPS * ROWS_HERE * HALVES * HALF
FACTOR = HDIM**-0.5
LOG2E = 1.4426950408889634


def dot(a, b, ca, cb):
    return lax.dot_general(a, b, (((ca,), (cb,)), ((), ())), preferred_element_type=F32)


def rows_of(block):
    return block.reshape(-1, HDIM)


def kernel(
    q, k, v, g, dq_out, dk_out, dv_out, got, made, key_total, value_total, key_t, weights, products,
    in_sem, in_send, out_sem, out_send,
):
    win = lax.axis_index("win")
    seq = lax.axis_index("seq")
    group, member = lax.div(seq, MEMBERS), lax.rem(seq, MEMBERS)
    core = lax.rem(member, 2)

    def place_of(window, head_core):
        return window + head_core * (1 - 2 * lax.rem(window, 2))

    work = place_of(win, core)
    work_east = lax.rem(work + 1, WINS)
    west = lax.rem(win + WINS - 1, WINS)
    stays = core == 0
    stays_west = (core == 1) & (lax.rem(win, 2) == 1)

    barrier = pltpu.get_barrier_semaphore()

    def greet(n, carry):
        peer = lax.rem(seq + n, SEQS)
        peer_core = lax.rem(peer, 2)
        far = (n > 0) | jnp.logical_not(stays)
        far_west = (n > 0) | jnp.logical_not(stays_west)

        @pl.when(far)
        def _():
            for place in (place_of(win, peer_core), work):
                pl.semaphore_signal(barrier, inc=1, device_id={"win": place, "seq": peer}, device_id_type=MESH)

        @pl.when(far_west)
        def _():
            for place in (place_of(west, peer_core), work_east):
                pl.semaphore_signal(barrier, inc=1, device_id={"win": place, "seq": peer}, device_id_type=MESH)

        return carry

    lax.fori_loop(0, SEQS, greet, 0)

    @pl.when(stays | stays_west)
    def _():
        pl.semaphore_wait(barrier, 4 * SEQS - 2)

    @pl.when(jnp.logical_not(stays | stays_west))
    def _():
        pl.semaphore_wait(barrier, 4 * SEQS)

    def send(src, dst, send_sem, recv_sem, to_win, to_seq):
        pltpu.make_async_remote_copy(
            src_ref=src,
            dst_ref=dst,
            send_sem=send_sem,
            recv_sem=recv_sem,
            device_id={"win": to_win, "seq": to_seq},
            device_id_type=MESH,
        ).start()

    def peer_at(n):
        over = lax.rem(n + 1, 4)
        across = lax.rem(n + lax.div(n, 4), 2)
        core = 1 - lax.div(n, 8)
        to_group = lax.rem(group + over, GROUPS)
        to_high = lax.rem(lax.div(member, 2) + across, 2)
        to_core = lax.rem(lax.rem(member, 2) + core, 2)
        return to_group * MEMBERS + to_high * 2 + to_core

    moved_group = lax.rem(group + 2, GROUPS)

    def send_inputs(b, first, last):
        def step(n, carry):
            peer = peer_at(n)
            peer_core = lax.rem(peer, 2)
            columns = pl.ds(pl.multiple_of(peer * HDIM, HDIM), HDIM)

            @pl.when((n < SEQS - 1) | jnp.logical_not(stays_west))
            def _():
                send(
                    g.at[b, :, 0, :, columns],
                    got.at[b, 3, moved_group, member, :, 1],
                    in_send.at[b, 4],
                    in_sem.at[b],
                    place_of(west, peer_core),
                    peer,
                )

            @pl.when((n < SEQS - 1) | jnp.logical_not(stays))
            def _():
                place = place_of(win, peer_core)
                for a, array in enumerate((q, k, v)):
                    send(
                        array.at[b, :, :, :, columns],
                        got.at[b, a, group, member],
                        in_send.at[b, a],
                        in_sem.at[b],
                        place,
                        peer,
                    )
                send(
                    g.at[b, :, 1, :, columns],
                    got.at[b, 3, moved_group, member, :, 0],
                    in_send.at[b, 3],
                    in_sem.at[b],
                    place,
                    peer,
                )

            return carry

        lax.fori_loop(first, last, step, 0)

    def own_inputs(b):
        columns = pl.ds(pl.multiple_of(seq * HDIM, HDIM), HDIM)

        @pl.when(stays)
        def _():
            for a, array in enumerate((q, k, v)):
                pltpu.make_async_copy(
                    array.at[b, :, :, :, columns], got.at[b, a, group, member], in_sem.at[b]
                ).start()
            pltpu.make_async_copy(
                g.at[b, :, 1, :, columns], got.at[b, 3, moved_group, member, :, 0], in_sem.at[b]
            ).start()

        @pl.when(stays_west)
        def _():
            pltpu.make_async_copy(
                g.at[b, :, 0, :, columns], got.at[b, 3, moved_group, member, :, 1], in_sem.at[b]
            ).start()

    my_columns = pl.ds(pl.multiple_of(seq * HDIM, HDIM), HDIM)
    outs = (dq_out, dk_out, dv_out)

    def send_gradient(b, a, to_group, to_member):
        peer = to_group * MEMBERS + to_member
        at_group = lax.rem(to_group + 2, GROUPS)
        parts = (
            (1, outs[a].at[b, :, 0, :, my_columns], work_east, (peer == seq) & stays_west),
            (0, outs[a].at[b, :, 1, :, my_columns], work, (peer == seq) & stays),
        )
        for half, place, to_win, at_home in parts:
            part = made.at[b, a, at_group, to_member, :, half]

            @pl.when(jnp.logical_not(at_home))
            def _():
                send(part, place, out_send.at[b, a, half], out_sem.at[a], to_win, peer)

            @pl.when(at_home)
            def _():
                pltpu.make_async_copy(part, place, out_sem.at[a]).start()

    def grads(b):
        key_total[...] = jnp.zeros_like(key_total)
        value_total[...] = jnp.zeros_like(value_total)
        key_t[...] = rows_of(got[b, 1]).T

        def block(j, carry):
            @pl.when((b == 0) & (j == 0))
            def _():
                send_inputs(1, SEQS // 2, SEQS)

            query = rows_of(got[b, 0, :, j])
            grad = rows_of(got[b, 3, :, j])
            top = jnp.full((8, CHUNK), -jnp.inf, F32)
            for i in range(TOKENS // CHUNK):
                keys = pl.ds(i * CHUNK, CHUNK)
                scores = dot(rows_of(got[b, 1, i]), query, 1, 1)
                weights[keys] = scores
                top = jnp.maximum(top, jnp.max(scores.reshape(-1, 8, CHUNK), axis=0))
            top = jnp.max(top, axis=0, keepdims=True) * (FACTOR * LOG2E)
            total = jnp.zeros((8, CHUNK), F32)
            row_dot = jnp.zeros((8, CHUNK), F32)
            for i in range(TOKENS // CHUNK):
                keys = pl.ds(i * CHUNK, CHUNK)
                weight = jnp.exp2(weights[keys] * (FACTOR * LOG2E) - top)
                product = weight * dot(rows_of(got[b, 2, i]), grad, 1, 1)
                total = total + jnp.sum(weight.reshape(-1, 8, CHUNK), axis=0)
                row_dot = row_dot + jnp.sum(product.reshape(-1, 8, CHUNK), axis=0)
                weights[keys] = weight
                products[keys] = product
            share = 1.0 / jnp.sum(total, axis=0, keepdims=True)
            row_dot = jnp.sum(row_dot, axis=0, keepdims=True) * share * share
            query_grad = jnp.zeros((HDIM, CHUNK), F32)
            for i in range(TOKENS // CHUNK):
                keys = pl.ds(i * CHUNK, CHUNK)
                weight = weights[keys]
                low = (weight * share).astype(BF16)
                score_grad = (products[keys] * share - weight * row_dot).astype(BF16)
                value_total[keys] += dot(low, grad, 1, 0)
                key_total[keys] += dot(score_grad, query, 1, 0)
                query_grad = query_grad + dot(key_t[:, keys], score_grad, 1, 0)
            made[b, 0, :, j] = (query_grad * FACTOR).T.astype(BF16).reshape(GROUPS, ROWS_HERE, HALVES, HALF, HDIM)
            for n in range(GROUPS):
                send_gradient(b, 0, lax.rem(group + n + 1, GROUPS), j)
            return carry

        lax.fori_loop(0, MEMBERS, block, 0)
        whole = (GROUPS, MEMBERS, ROWS_HERE, HALVES, HALF, HDIM)
        made[b, 1] = (key_total[...] * FACTOR).astype(BF16).reshape(whole)
        made[b, 2] = value_total[...].astype(BF16).reshape(whole)

        def step(n, carry):
            peer = peer_at(n)
            for a in (1, 2):
                send_gradient(b, a, lax.div(peer, MEMBERS), lax.rem(peer, MEMBERS))
            return carry

        lax.fori_loop(0, SEQS, step, 0)

    send_inputs(0, 0, SEQS)
    for b in range(SAMPLES):
        own_inputs(b)
    send_inputs(1, 0, SEQS // 2)

    def sample(b, carry):
        pltpu.make_async_copy(got.at[b], got.at[b], in_sem.at[b]).wait()
        grads(b)
        return carry

    lax.fori_loop(0, SAMPLES, sample, 0)

    for a in range(3):
        pltpu.make_async_copy(outs[a], outs[a], out_sem.at[a]).wait()

    def all_sent(whole, sem, one_stays):
        most = whole.at[..., pl.ds(0, (SEQS - 1) * HDIM)]

        @pl.when(one_stays)
        def _():
            pltpu.make_async_copy(most, most, sem).wait()

        @pl.when(jnp.logical_not(one_stays))
        def _():
            pltpu.make_async_copy(whole, whole, sem).wait()

    for b in range(SAMPLES):
        for a in range(3):
            all_sent(q.at[b], in_send.at[b, a], stays)
        all_sent(q.at[b, :, 0], in_send.at[b, 3], stays)
        all_sent(q.at[b, :, 0], in_send.at[b, 4], stays_west)
        for a in range(3):
            all_sent(q.at[b, :, 0], out_send.at[b, a, 0], stays)
            all_sent(q.at[b, :, 0], out_send.at[b, a, 1], stays_west)


def on_device(queries, key_states, value_states, out_grad):
    shape = (SAMPLES, ROWS_HERE, HALVES, HALF, D)
    arrays = [a.reshape(shape) for a in (queries, key_states, value_states, out_grad)]
    tokens = (GROUPS, MEMBERS, ROWS_HERE, HALVES, HALF, HDIM)
    results = pl.pallas_call(
        kernel,
        out_shape=[pltpu.VMEM(shape, BF16)] * 3,
        in_specs=[pl.BlockSpec(memory_space=pltpu.HBM)] * 4,
        out_specs=[pl.BlockSpec(memory_space=pltpu.VMEM)] * 3,
        scratch_shapes=[
            pltpu.VMEM((SAMPLES, 4, *tokens), BF16),
            pltpu.VMEM((SAMPLES, 3, *tokens), BF16),
            pltpu.VMEM((TOKENS, HDIM), F32),
            pltpu.VMEM((TOKENS, HDIM), F32),
            pltpu.VMEM((HDIM, TOKENS), BF16),
            pltpu.VMEM((TOKENS, CHUNK), F32),
            pltpu.VMEM((TOKENS, CHUNK), F32),
            pltpu.SemaphoreType.DMA((SAMPLES,)),
            pltpu.SemaphoreType.DMA((SAMPLES, 5)),
            pltpu.SemaphoreType.DMA((3,)),
            pltpu.SemaphoreType.DMA((SAMPLES, 3, 2)),
        ],
        compiler_params=pltpu.CompilerParams(collective_id=0, has_side_effects=True, vmem_limit_bytes=58 * 2**20),
        cost_estimate=pl.CostEstimate(flops=10 * 2 * TOKENS * TOKENS * HDIM, bytes_accessed=7 * 2**20, transcendentals=2 * TOKENS * TOKENS),
        name="window_backward",
    )(*arrays)
    return tuple(r.reshape(queries.shape) for r in results)


def solution(mesh):
    spec = P(None, "win", "seq", None)
    return jax.shard_map(on_device, mesh=mesh, in_specs=(spec,) * 4, out_specs=(spec,) * 3, check_vma=False)
```

```python
import jax
import jax.numpy as jnp
from jax import lax
from jax.experimental import pallas as pl
from jax.experimental.pallas import tpu as pltpu
from jax.sharding import PartitionSpec as P

F32, BF16 = jnp.float32, jnp.bfloat16
MESH = pl.DeviceIdType.MESH
SAMPLES, HEADS, HDIM, D = 2, 16, 128, 2048
WINS, SEQS = 16, 16
TOKENS = 2048
GROUPS, MEMBERS = 4, 4
ROWS_HERE, HALVES, HALF = 2, 2, 32
CHUNK = GROUPS * ROWS_HERE * HALVES * HALF
FACTOR = HDIM**-0.5
LOG2E = 1.4426950408889634


def dot(a, b, ca, cb):
    return lax.dot_general(a, b, (((ca,), (cb,)), ((), ())), preferred_element_type=F32)


def rows_of(block):
    return block.reshape(-1, HDIM)


def kernel(
    q, k, v, g, dq_out, dk_out, dv_out, got, made, key_total, value_total, key_t, weights, products,
    in_sem, in_send, out_sem, out_send,
):
    win = lax.axis_index("win")
    seq = lax.axis_index("seq")
    group, member = lax.div(seq, MEMBERS), lax.rem(seq, MEMBERS)
    core = lax.rem(member, 2)

    def place_of(window, head_core):
        return window + head_core * (1 - 2 * lax.rem(window, 2))

    work = place_of(win, core)
    work_east = lax.rem(work + 1, WINS)
    west = lax.rem(win + WINS - 1, WINS)
    stays = core == 0
    stays_west = (core == 1) & (lax.rem(win, 2) == 1)

    barrier = pltpu.get_barrier_semaphore()

    def greet(n, carry):
        peer = lax.rem(seq + n, SEQS)
        peer_core = lax.rem(peer, 2)
        far = (n > 0) | jnp.logical_not(stays)
        far_west = (n > 0) | jnp.logical_not(stays_west)

        @pl.when(far)
        def _():
            for place in (place_of(win, peer_core), work):
                pl.semaphore_signal(barrier, inc=1, device_id={"win": place, "seq": peer}, device_id_type=MESH)

        @pl.when(far_west)
        def _():
            for place in (place_of(west, peer_core), work_east):
                pl.semaphore_signal(barrier, inc=1, device_id={"win": place, "seq": peer}, device_id_type=MESH)

        return carry

    lax.fori_loop(0, SEQS, greet, 0)

    @pl.when(stays | stays_west)
    def _():
        pl.semaphore_wait(barrier, 4 * SEQS - 2)

    @pl.when(jnp.logical_not(stays | stays_west))
    def _():
        pl.semaphore_wait(barrier, 4 * SEQS)

    def send(src, dst, send_sem, recv_sem, to_win, to_seq):
        pltpu.make_async_remote_copy(
            src_ref=src,
            dst_ref=dst,
            send_sem=send_sem,
            recv_sem=recv_sem,
            device_id={"win": to_win, "seq": to_seq},
            device_id_type=MESH,
        ).start()

    def peer_at(n):
        over = lax.rem(n + 1, 4)
        across = lax.rem(n + lax.div(n, 4), 2)
        core = 1 - lax.div(n, 8)
        to_group = lax.rem(group + over, GROUPS)
        to_high = lax.rem(lax.div(member, 2) + across, 2)
        to_core = lax.rem(lax.rem(member, 2) + core, 2)
        return to_group * MEMBERS + to_high * 2 + to_core

    moved_group = lax.rem(group + 2, GROUPS)

    def send_inputs(b, first, last):
        def step(n, carry):
            peer = peer_at(n)
            peer_core = lax.rem(peer, 2)
            columns = pl.ds(pl.multiple_of(peer * HDIM, HDIM), HDIM)

            @pl.when((n < SEQS - 1) | jnp.logical_not(stays_west))
            def _():
                send(
                    g.at[b, :, 0, :, columns],
                    got.at[b, 3, moved_group, member, :, 1],
                    in_send.at[b, 4],
                    in_sem.at[b],
                    place_of(west, peer_core),
                    peer,
                )

            @pl.when((n < SEQS - 1) | jnp.logical_not(stays))
            def _():
                place = place_of(win, peer_core)
                for a, array in enumerate((q, k, v)):
                    send(
                        array.at[b, :, :, :, columns],
                        got.at[b, a, group, member],
                        in_send.at[b, a],
                        in_sem.at[b],
                        place,
                        peer,
                    )
                send(
                    g.at[b, :, 1, :, columns],
                    got.at[b, 3, moved_group, member, :, 0],
                    in_send.at[b, 3],
                    in_sem.at[b],
                    place,
                    peer,
                )

            return carry

        lax.fori_loop(first, last, step, 0)

    def own_inputs(b):
        columns = pl.ds(pl.multiple_of(seq * HDIM, HDIM), HDIM)

        @pl.when(stays)
        def _():
            for a, array in enumerate((q, k, v)):
                pltpu.make_async_copy(
                    array.at[b, :, :, :, columns], got.at[b, a, group, member], in_sem.at[b]
                ).start()
            pltpu.make_async_copy(
                g.at[b, :, 1, :, columns], got.at[b, 3, moved_group, member, :, 0], in_sem.at[b]
            ).start()

        @pl.when(stays_west)
        def _():
            pltpu.make_async_copy(
                g.at[b, :, 0, :, columns], got.at[b, 3, moved_group, member, :, 1], in_sem.at[b]
            ).start()

    my_columns = pl.ds(pl.multiple_of(seq * HDIM, HDIM), HDIM)
    outs = (dq_out, dk_out, dv_out)

    def send_gradient(b, a, to_group, to_member):
        peer = to_group * MEMBERS + to_member
        at_group = lax.rem(to_group + 2, GROUPS)
        parts = (
            (1, outs[a].at[b, :, 0, :, my_columns], work_east, (peer == seq) & stays_west),
            (0, outs[a].at[b, :, 1, :, my_columns], work, (peer == seq) & stays),
        )
        for half, place, to_win, at_home in parts:
            part = made.at[b, a, at_group, to_member, :, half]

            @pl.when(jnp.logical_not(at_home))
            def _():
                send(part, place, out_send.at[b, a, half], out_sem.at[a], to_win, peer)

            @pl.when(at_home)
            def _():
                pltpu.make_async_copy(part, place, out_sem.at[a]).start()

    def send_totals(b, first, last):
        def step(n, carry):
            peer = peer_at(n)
            for a in (1, 2):
                send_gradient(b, a, lax.div(peer, MEMBERS), lax.rem(peer, MEMBERS))
            return carry

        lax.fori_loop(first, last, step, 0)

    def send_rows(b, to_member):
        for n in range(GROUPS):
            send_gradient(b, 0, lax.rem(group + n + 1, GROUPS), to_member)

    def grads(b):
        key_total[...] = jnp.zeros_like(key_total)
        value_total[...] = jnp.zeros_like(value_total)
        key_t[...] = rows_of(got[b, 1]).T

        def block(j, carry):
            @pl.when((b == 0) & (j == 0))
            def _():
                send_inputs(1, SEQS // 2, SEQS)

            @pl.when(b == 1)
            def _():
                send_totals(0, j * 4, (j + 1) * 4)

            query = rows_of(got[b, 0, :, j])
            grad = rows_of(got[b, 3, :, j])
            top = jnp.full((8, CHUNK), -jnp.inf, F32)
            for i in range(TOKENS // CHUNK):
                keys = pl.ds(i * CHUNK, CHUNK)
                scores = dot(rows_of(got[b, 1, i]), query, 1, 1)
                weights[keys] = scores
                top = jnp.maximum(top, jnp.max(scores.reshape(-1, 8, CHUNK), axis=0))
            top = jnp.max(top, axis=0, keepdims=True) * (FACTOR * LOG2E)
            total = jnp.zeros((8, CHUNK), F32)
            row_dot = jnp.zeros((8, CHUNK), F32)
            for i in range(TOKENS // CHUNK):
                keys = pl.ds(i * CHUNK, CHUNK)
                weight = jnp.exp2(weights[keys] * (FACTOR * LOG2E) - top)
                product = weight * dot(rows_of(got[b, 2, i]), grad, 1, 1)
                total = total + jnp.sum(weight.reshape(-1, 8, CHUNK), axis=0)
                row_dot = row_dot + jnp.sum(product.reshape(-1, 8, CHUNK), axis=0)
                weights[keys] = weight
                products[keys] = product

            @pl.when(j > 0)
            def _():
                send_rows(b, j - 1)

            share = 1.0 / jnp.sum(total, axis=0, keepdims=True)
            row_dot = jnp.sum(row_dot, axis=0, keepdims=True) * share * share
            query_grad = jnp.zeros((HDIM, CHUNK), F32)
            for i in range(TOKENS // CHUNK):
                keys = pl.ds(i * CHUNK, CHUNK)
                weight = weights[keys]
                low = (weight * share).astype(BF16)
                score_grad = (products[keys] * share - weight * row_dot).astype(BF16)
                value_total[keys] += dot(low, grad, 1, 0)
                key_total[keys] += dot(score_grad, query, 1, 0)
                query_grad = query_grad + dot(key_t[:, keys], score_grad, 1, 0)
            made[b, 0, :, j] = (query_grad * FACTOR).T.astype(BF16).reshape(GROUPS, ROWS_HERE, HALVES, HALF, HDIM)
            @pl.when(j == MEMBERS - 1)
            def _():
                send_rows(b, j)

            return carry

        lax.fori_loop(0, MEMBERS, block, 0)
        whole = (GROUPS, MEMBERS, ROWS_HERE, HALVES, HALF, HDIM)
        made[b, 1] = (key_total[...] * FACTOR).astype(BF16).reshape(whole)
        made[b, 2] = value_total[...].astype(BF16).reshape(whole)

        @pl.when(b == 1)
        def _():
            send_totals(1, 0, SEQS)

    send_inputs(0, 0, SEQS)
    for b in range(SAMPLES):
        own_inputs(b)
    send_inputs(1, 0, SEQS // 2)

    def sample(b, carry):
        pltpu.make_async_copy(got.at[b], got.at[b], in_sem.at[b]).wait()
        grads(b)
        return carry

    lax.fori_loop(0, SAMPLES, sample, 0)

    for a in range(3):
        pltpu.make_async_copy(outs[a], outs[a], out_sem.at[a]).wait()

    def all_sent(whole, sem, one_stays):
        most = whole.at[..., pl.ds(0, (SEQS - 1) * HDIM)]

        @pl.when(one_stays)
        def _():
            pltpu.make_async_copy(most, most, sem).wait()

        @pl.when(jnp.logical_not(one_stays))
        def _():
            pltpu.make_async_copy(whole, whole, sem).wait()

    for b in range(SAMPLES):
        for a in range(3):
            all_sent(q.at[b], in_send.at[b, a], stays)
        all_sent(q.at[b, :, 0], in_send.at[b, 3], stays)
        all_sent(q.at[b, :, 0], in_send.at[b, 4], stays_west)
        for a in range(3):
            all_sent(q.at[b, :, 0], out_send.at[b, a, 0], stays)
            all_sent(q.at[b, :, 0], out_send.at[b, a, 1], stays_west)


def on_device(queries, key_states, value_states, out_grad):
    shape = (SAMPLES, ROWS_HERE, HALVES, HALF, D)
    arrays = [a.reshape(shape) for a in (queries, key_states, value_states, out_grad)]
    tokens = (GROUPS, MEMBERS, ROWS_HERE, HALVES, HALF, HDIM)
    results = pl.pallas_call(
        kernel,
        out_shape=[pltpu.VMEM(shape, BF16)] * 3,
        in_specs=[pl.BlockSpec(memory_space=pltpu.HBM)] * 4,
        out_specs=[pl.BlockSpec(memory_space=pltpu.VMEM)] * 3,
        scratch_shapes=[
            pltpu.VMEM((SAMPLES, 4, *tokens), BF16),
            pltpu.VMEM((SAMPLES, 3, *tokens), BF16),
            pltpu.VMEM((TOKENS, HDIM), F32),
            pltpu.VMEM((TOKENS, HDIM), F32),
            pltpu.VMEM((HDIM, TOKENS), BF16),
            pltpu.VMEM((TOKENS, CHUNK), F32),
            pltpu.VMEM((TOKENS, CHUNK), F32),
            pltpu.SemaphoreType.DMA((SAMPLES,)),
            pltpu.SemaphoreType.DMA((SAMPLES, 5)),
            pltpu.SemaphoreType.DMA((3,)),
            pltpu.SemaphoreType.DMA((SAMPLES, 3, 2)),
        ],
        compiler_params=pltpu.CompilerParams(collective_id=0, has_side_effects=True, vmem_limit_bytes=58 * 2**20),
        cost_estimate=pl.CostEstimate(flops=10 * 2 * TOKENS * TOKENS * HDIM, bytes_accessed=7 * 2**20, transcendentals=2 * TOKENS * TOKENS),
        name="window_backward",
    )(*arrays)
    return tuple(r.reshape(queries.shape) for r in results)


def solution(mesh):
    spec = P(None, "win", "seq", None)
    return jax.shard_map(on_device, mesh=mesh, in_specs=(spec,) * 4, out_specs=(spec,) * 3, check_vma=False)
```

```python
import jax
import jax.numpy as jnp
from jax import lax
from jax.experimental import pallas as pl
from jax.experimental.pallas import tpu as pltpu
from jax.sharding import PartitionSpec as P

F32, BF16 = jnp.float32, jnp.bfloat16
MESH = pl.DeviceIdType.MESH
SAMPLES, HEADS, HDIM, D = 2, 16, 128, 2048
WINS, SEQS = 16, 16
TOKENS = 2048
GROUPS, MEMBERS = 4, 4
ROWS_HERE, HALVES, HALF = 2, 2, 32
CHUNK = GROUPS * ROWS_HERE * HALVES * HALF
FACTOR = HDIM**-0.5
LOG2E = 1.4426950408889634


def dot(a, b, ca, cb):
    return lax.dot_general(a, b, (((ca,), (cb,)), ((), ())), preferred_element_type=F32)


def rows_of(block):
    return block.reshape(-1, HDIM)


def kernel(
    q, k, v, g, dq_out, dk_out, dv_out, got, made, key_total, value_total, key_t, weights, products,
    in_sem, in_send, out_sem, out_send,
):
    win = lax.axis_index("win")
    seq = lax.axis_index("seq")
    group, member = lax.div(seq, MEMBERS), lax.rem(seq, MEMBERS)
    core = lax.rem(member, 2)

    def place_of(window, head_core):
        return window + head_core * (1 - 2 * lax.rem(window, 2))

    work = place_of(win, core)
    work_east = lax.rem(work + 1, WINS)
    west = lax.rem(win + WINS - 1, WINS)
    stays = core == 0
    stays_west = (core == 1) & (lax.rem(win, 2) == 1)

    barrier = pltpu.get_barrier_semaphore()

    def greet(n, carry):
        peer = lax.rem(seq + n, SEQS)
        peer_core = lax.rem(peer, 2)
        far = (n > 0) | jnp.logical_not(stays)
        far_west = (n > 0) | jnp.logical_not(stays_west)

        @pl.when(far)
        def _():
            for place in (place_of(win, peer_core), work):
                pl.semaphore_signal(barrier, inc=1, device_id={"win": place, "seq": peer}, device_id_type=MESH)

        @pl.when(far_west)
        def _():
            for place in (place_of(west, peer_core), work_east):
                pl.semaphore_signal(barrier, inc=1, device_id={"win": place, "seq": peer}, device_id_type=MESH)

        return carry

    lax.fori_loop(0, SEQS, greet, 0)

    @pl.when(stays | stays_west)
    def _():
        pl.semaphore_wait(barrier, 4 * SEQS - 2)

    @pl.when(jnp.logical_not(stays | stays_west))
    def _():
        pl.semaphore_wait(barrier, 4 * SEQS)

    def send(src, dst, send_sem, recv_sem, to_win, to_seq):
        pltpu.make_async_remote_copy(
            src_ref=src,
            dst_ref=dst,
            send_sem=send_sem,
            recv_sem=recv_sem,
            device_id={"win": to_win, "seq": to_seq},
            device_id_type=MESH,
        ).start()

    def peer_at(n):
        over = lax.rem(n + 1, 4)
        across = lax.rem(n + lax.div(n, 4), 2)
        core = 1 - lax.div(n, 8)
        to_group = lax.rem(group + over, GROUPS)
        to_high = lax.rem(lax.div(member, 2) + across, 2)
        to_core = lax.rem(lax.rem(member, 2) + core, 2)
        return to_group * MEMBERS + to_high * 2 + to_core

    moved_group = lax.rem(group + 2, GROUPS)

    def send_inputs(b, first, last):
        def step(n, carry):
            peer = peer_at(n)
            peer_core = lax.rem(peer, 2)
            columns = pl.ds(pl.multiple_of(peer * HDIM, HDIM), HDIM)

            @pl.when((n < SEQS - 1) | jnp.logical_not(stays_west))
            def _():
                send(
                    g.at[b, :, 0, :, columns],
                    got.at[b, 3, moved_group, member, :, 1],
                    in_send.at[b, 4],
                    in_sem.at[b],
                    place_of(west, peer_core),
                    peer,
                )

            @pl.when((n < SEQS - 1) | jnp.logical_not(stays))
            def _():
                place = place_of(win, peer_core)
                for a, array in enumerate((q, k, v)):
                    send(
                        array.at[b, :, :, :, columns],
                        got.at[b, a, group, member],
                        in_send.at[b, a],
                        in_sem.at[b],
                        place,
                        peer,
                    )
                send(
                    g.at[b, :, 1, :, columns],
                    got.at[b, 3, moved_group, member, :, 0],
                    in_send.at[b, 3],
                    in_sem.at[b],
                    place,
                    peer,
                )

            return carry

        lax.fori_loop(first, last, step, 0)

    def own_inputs(b):
        columns = pl.ds(pl.multiple_of(seq * HDIM, HDIM), HDIM)

        @pl.when(stays)
        def _():
            for a, array in enumerate((q, k, v)):
                pltpu.make_async_copy(
                    array.at[b, :, :, :, columns], got.at[b, a, group, member], in_sem.at[b]
                ).start()
            pltpu.make_async_copy(
                g.at[b, :, 1, :, columns], got.at[b, 3, moved_group, member, :, 0], in_sem.at[b]
            ).start()

        @pl.when(stays_west)
        def _():
            pltpu.make_async_copy(
                g.at[b, :, 0, :, columns], got.at[b, 3, moved_group, member, :, 1], in_sem.at[b]
            ).start()

    my_columns = pl.ds(pl.multiple_of(seq * HDIM, HDIM), HDIM)
    outs = (dq_out, dk_out, dv_out)

    def send_gradient(b, a, to_group, to_member):
        peer = to_group * MEMBERS + to_member
        at_group = lax.rem(to_group + 2, GROUPS)
        parts = (
            (1, outs[a].at[b, :, 0, :, my_columns], work_east, (peer == seq) & stays_west),
            (0, outs[a].at[b, :, 1, :, my_columns], work, (peer == seq) & stays),
        )
        for half, place, to_win, at_home in parts:
            part = made.at[b, a, at_group, to_member, :, half]

            @pl.when(jnp.logical_not(at_home))
            def _():
                send(part, place, out_send.at[b, a, half], out_sem.at[a], to_win, peer)

            @pl.when(at_home)
            def _():
                pltpu.make_async_copy(part, place, out_sem.at[a]).start()

    def send_totals(b, first, last):
        def step(n, carry):
            peer = peer_at(n)
            for a in (1, 2):
                send_gradient(b, a, lax.div(peer, MEMBERS), lax.rem(peer, MEMBERS))
            return carry

        lax.fori_loop(first, last, step, 0)

    def send_rows(b, to_member):
        for n in range(GROUPS):
            send_gradient(b, 0, lax.rem(group + n + 1, GROUPS), to_member)

    def grads(b):
        key_total[...] = jnp.zeros_like(key_total)
        value_total[...] = jnp.zeros_like(value_total)
        key_t[...] = rows_of(got[b, 1]).T

        def block(j, carry):
            @pl.when((b == 0) & (j == 0))
            def _():
                send_inputs(1, SEQS // 2, SEQS)

            @pl.when(b == 1)
            def _():
                send_totals(0, j * 4, (j + 1) * 4)

            query = rows_of(got[b, 0, :, j])
            grad = rows_of(got[b, 3, :, j])
            top = jnp.full((8, CHUNK), -jnp.inf, F32)
            for i in range(TOKENS // CHUNK):
                keys = pl.ds(i * CHUNK, CHUNK)
                scores = dot(rows_of(got[b, 1, i]), query, 1, 1)
                weights[keys] = scores
                top = jnp.maximum(top, jnp.max(scores.reshape(-1, 8, CHUNK), axis=0))
            top = jnp.max(top, axis=0, keepdims=True) * (FACTOR * LOG2E)
            total = jnp.zeros((8, CHUNK), F32)
            row_dot = jnp.zeros((8, CHUNK), F32)
            for i in range(TOKENS // CHUNK):
                keys = pl.ds(i * CHUNK, CHUNK)
                weight = jnp.exp2(weights[keys] * (FACTOR * LOG2E) - top)
                product = weight * dot(rows_of(got[b, 2, i]), grad, 1, 1)
                total = total + jnp.sum(weight.reshape(-1, 8, CHUNK), axis=0)
                row_dot = row_dot + jnp.sum(product.reshape(-1, 8, CHUNK), axis=0)
                weights[keys] = weight
                products[keys] = product

            @pl.when(j > 0)
            def _():
                send_rows(b, j - 1)

            share = 1.0 / jnp.sum(total, axis=0, keepdims=True)
            row_dot = jnp.sum(row_dot, axis=0, keepdims=True) * share * share
            query_grad = jnp.zeros((HDIM, CHUNK), F32)
            for i in range(TOKENS // CHUNK):
                keys = pl.ds(i * CHUNK, CHUNK)
                weight = weights[keys]
                low = (weight * share).astype(BF16)
                score_grad = (products[keys] * share - weight * row_dot).astype(BF16)
                value_total[keys] += dot(low, grad, 1, 0)
                key_total[keys] += dot(score_grad, query, 1, 0)
                query_grad = query_grad + dot(key_t[:, keys], score_grad, 1, 0)
            made[b, 0, :, j] = (query_grad * FACTOR).T.astype(BF16).reshape(GROUPS, ROWS_HERE, HALVES, HALF, HDIM)
            @pl.when(j == MEMBERS - 1)
            def _():
                send_rows(b, j)

            return carry

        lax.fori_loop(0, MEMBERS, block, 0)
        whole = (GROUPS, MEMBERS, ROWS_HERE, HALVES, HALF, HDIM)
        made[b, 1] = (key_total[...] * FACTOR).astype(BF16).reshape(whole)
        made[b, 2] = value_total[...].astype(BF16).reshape(whole)

        @pl.when(b == 1)
        def _():
            send_totals(1, 0, SEQS)

    send_inputs(0, 0, SEQS)
    for b in range(SAMPLES):
        own_inputs(b)
    send_inputs(1, 0, SEQS // 2)

    def sample(b, carry):
        pltpu.make_async_copy(got.at[b], got.at[b], in_sem.at[b]).wait()
        grads(b)
        return carry

    lax.fori_loop(0, SAMPLES, sample, 0)

    for a in range(3):
        pltpu.make_async_copy(outs[a], outs[a], out_sem.at[a]).wait()

    def all_sent(whole, sem, one_stays):
        most = whole.at[..., pl.ds(0, (SEQS - 1) * HDIM)]

        @pl.when(one_stays)
        def _():
            pltpu.make_async_copy(most, most, sem).wait()

        @pl.when(jnp.logical_not(one_stays))
        def _():
            pltpu.make_async_copy(whole, whole, sem).wait()

    for b in range(SAMPLES):
        for a in range(3):
            all_sent(q.at[b], in_send.at[b, a], stays)
        all_sent(q.at[b, :, 0], in_send.at[b, 3], stays)
        all_sent(q.at[b, :, 0], in_send.at[b, 4], stays_west)
        for a in range(3):
            all_sent(q.at[b, :, 0], out_send.at[b, a, 0], stays)
            all_sent(q.at[b, :, 0], out_send.at[b, a, 1], stays_west)


def settle(*refs):
    ins, outs, sem = refs[:3], refs[3:6], refs[6]
    copies = [
        pltpu.make_async_copy(a.at[b], o.at[b], sem.at[i, b])
        for i, (a, o) in enumerate(zip(ins, outs))
        for b in range(SAMPLES)
    ]
    for copy in copies:
        copy.start()
    for copy in copies:
        copy.wait()


def on_device(queries, key_states, value_states, out_grad):
    shape = (SAMPLES, ROWS_HERE, HALVES, HALF, D)
    arrays = [a.reshape(shape) for a in (queries, key_states, value_states, out_grad)]
    tokens = (GROUPS, MEMBERS, ROWS_HERE, HALVES, HALF, HDIM)
    results = pl.pallas_call(
        kernel,
        out_shape=[pltpu.VMEM(shape, BF16)] * 3,
        in_specs=[pl.BlockSpec(memory_space=pltpu.HBM)] * 4,
        out_specs=[pl.BlockSpec(memory_space=pltpu.VMEM)] * 3,
        scratch_shapes=[
            pltpu.VMEM((SAMPLES, 4, *tokens), BF16),
            pltpu.VMEM((SAMPLES, 3, *tokens), BF16),
            pltpu.VMEM((TOKENS, HDIM), F32),
            pltpu.VMEM((TOKENS, HDIM), F32),
            pltpu.VMEM((HDIM, TOKENS), BF16),
            pltpu.VMEM((TOKENS, CHUNK), F32),
            pltpu.VMEM((TOKENS, CHUNK), F32),
            pltpu.SemaphoreType.DMA((SAMPLES,)),
            pltpu.SemaphoreType.DMA((SAMPLES, 5)),
            pltpu.SemaphoreType.DMA((3,)),
            pltpu.SemaphoreType.DMA((SAMPLES, 3, 2)),
        ],
        compiler_params=pltpu.CompilerParams(collective_id=0, has_side_effects=True, vmem_limit_bytes=58 * 2**20),
        cost_estimate=pl.CostEstimate(flops=10 * 2 * TOKENS * TOKENS * HDIM, bytes_accessed=7 * 2**20, transcendentals=2 * TOKENS * TOKENS),
        name="window_backward",
    )(*arrays)
    results = pl.pallas_call(
        settle,
        out_shape=[jax.ShapeDtypeStruct(shape, BF16)] * 3,
        in_specs=[pl.BlockSpec(memory_space=pltpu.VMEM)] * 3,
        out_specs=[pl.BlockSpec(memory_space=pltpu.HBM)] * 3,
        scratch_shapes=[pltpu.SemaphoreType.DMA((3, SAMPLES))],
        compiler_params=pltpu.CompilerParams(vmem_limit_bytes=8 * 2**20),
        name="settle",
    )(*results)
    return tuple(r.reshape(queries.shape) for r in results)


def solution(mesh):
    spec = P(None, "win", "seq", None)
    return jax.shard_map(on_device, mesh=mesh, in_specs=(spec,) * 4, out_specs=(spec,) * 3, check_vma=False)
```
